128 devices in a mesh: grp: 4 (over z), shard: 32 (over x, y, core).
Axes of the slice: x: 4, y: 4, z: 4, core: 2. Of those that a mesh axis runs over, the one named last changes fastest.
Arguments:
- queries: bfloat16 [256, 4, 128, 128], P(('grp', 'shard')), may hold values from -40 to 40
- prefix_keys: bfloat16 [16, 32, 1024, 128], P('grp', 'shard'), may hold values from -6 to 6
- prefix_values: bfloat16 [16, 32, 1024, 128], P('grp', 'shard'), may hold values from -6 to 6
- suffix_keys: bfloat16 [256, 512, 8, 128], P(('grp', 'shard')), may hold values from -6 to 6
- suffix_values: bfloat16 [256, 512, 8, 128], P(('grp', 'shard')), may hold values from -6 to 6
- new_keys: bfloat16 [256, 4, 8, 128], P(('grp', 'shard')), may hold values from -6 to 6
- new_values: bfloat16 [256, 4, 8, 128], P(('grp', 'shard')), may hold values from -6 to 6
- suffix_lengths: int32 [256], P(('grp', 'shard')), may hold values from 64 to 512
- branch_prefix: int32 [256], P(('grp', 'shard')), may hold values from 0 to 15, as said below
- prefix_slot: int32 [16], replicated, may hold values from 0 to 15, as said below
Outputs:
- attended: bfloat16 [256, 4, 128, 128], P(('grp', 'shard'))
The draws below stay inside these ranges and needn't reach their ends.
Inputs may be any that keep to these rules, and one draw needn't show every extreme that they name: `branch_prefix`: slot s lies on group s // 4. Among the 2 branches of one device (aligned blocks of 2), at most 1 have prefixes whose slots lie in one group, and in every block some group has exactly 1. `prefix_slot`: each prefix has a slot of its own.
All inputs are finite; a program needn't handle non-finite values.
Results may differ from the reference program's by a relative error of at most 0.0056.
Values may be sent and summed in bfloat16 or wider, within the bound.
A program may use at most 64 MiB of HBM per device.

```python
import jax
import jax.numpy as jnp
from jax import lax

HEADS = 128
KVH = 8
HD = 128
STEPS = 4
NPREF = 16
BR_DEV = 2
BLK = 1024
SUF = 512
HPK = 16
TB = 4
SPG = 4
CAP = 1
BRANCHES = 256
N_GRP = 4
N_SHARD = 32
DEVICES = 128


def routing(key):
    key = jax.random.fold_in(key, 101)
    pieces = jax.random.split(key, 5)
    slot_of = jax.random.permutation(pieces[0], NPREF).astype(jnp.int32)
    prefix_at = jnp.argsort(slot_of).astype(jnp.int32)
    group_order = jax.random.permutation(pieces[1], N_GRP).astype(jnp.int32)
    picked = jax.random.randint(pieces[2], (DEVICES,), 0, 20)
    level = (picked >= 17).astype(jnp.int32) + (picked >= 18).astype(jnp.int32) + (picked >= 19).astype(jnp.int32)
    hottest = group_order[level]
    others = jax.random.randint(pieces[3], (DEVICES, BR_DEV), 1, N_GRP)
    position = jnp.arange(BR_DEV, dtype=jnp.int32)
    group_of = jnp.where(position[None, :] < CAP, hottest[:, None], (hottest[:, None] + others) % N_GRP)
    member = jax.random.randint(pieces[4], (DEVICES, BR_DEV), 0, SPG)
    chosen_prefix = prefix_at[group_of * SPG + member].reshape(BRANCHES)
    return (slot_of, chosen_prefix.astype(jnp.int32))


def draw_prefix_slot(key, part):
    slot_of, chosen_prefix = routing(key)
    return slot_of


def draw_branch_prefix(key, part):
    slot_of, chosen_prefix = routing(key)
    return chosen_prefix


def draw_prefix_keys(key, part):
    own_key = jax.random.fold_in(key, 3)
    return jnp.clip(jax.random.normal(own_key, (NPREF, N_SHARD, BLK, HD)), -6.0, 6.0).astype(jnp.bfloat16)


def draw_queries(key, part):
    own_key = jax.random.fold_in(key, 5)
    pieces = jax.random.split(own_key, 1)
    array_shape = (BRANCHES, STEPS, HEADS, HD)
    return jnp.clip(jax.random.normal(pieces[0], array_shape), -6.0, 6.0).astype(jnp.bfloat16)


def touch_ends(values, key, low, high):
    spot = [jax.random.randint(jax.random.fold_in(key, axis), (), 0, length) for axis, length in enumerate(values.shape)]
    longest = values.shape.index(max(values.shape))
    beside = spot[:longest] + [(spot[longest] + 1) % values.shape[longest]] + spot[longest + 1:]
    return values.at[tuple(spot)].set(low).at[tuple(beside)].set(high)


def block_levels(key, shape, shards, least, high):
    gain = 1.0
    for dim, shards_of in shards:
        steps = jax.random.uniform(jax.random.fold_in(jax.random.fold_in(key, 6), dim), (shards_of,), jnp.float32, least / len(shards), high / len(shards))
        gain = gain * jnp.repeat(jnp.exp(steps), shape[dim] // shards_of).reshape((-1,) + (1,) * (len(shape) - 1 - dim))
    return gain


def bell_draw(stream_key, extent, scale, limit, cuts=(), kind=jnp.bfloat16):
    values = scale * jax.random.normal(stream_key, extent, jnp.float32)
    if cuts:
        values = values * block_levels(stream_key, extent, cuts, -0.22, 0.18)
    return jnp.clip(values, -limit, limit).astype(kind)


def setup_inputs(seed: int = 0) -> dict:
    key_of = jax.random.split(jax.random.key(seed), 11)
    return {
        "queries": draw_queries(jax.random.fold_in(key_of[10], 71), 0),
        "prefix_keys": draw_prefix_keys(jax.random.fold_in(key_of[10], 71), 0),
        "prefix_values": bell_draw(key_of[2], (NPREF, N_SHARD, BLK, HD), 1.0, 6.0, ((0, 4), (1, 32))),
        "suffix_keys": bell_draw(key_of[3], (BRANCHES, SUF, KVH, HD), 1.0, 6.0, ((0, 128),)),
        "suffix_values": bell_draw(key_of[4], (BRANCHES, SUF, KVH, HD), 1.0, 6.0, ((0, 128),)),
        "new_keys": bell_draw(key_of[5], (BRANCHES, STEPS, KVH, HD), 1.0, 6.0, ((0, 128),)),
        "new_values": bell_draw(key_of[6], (BRANCHES, STEPS, KVH, HD), 1.0, 6.0, ((0, 128),)),
        "suffix_lengths": touch_ends(jax.random.randint(key_of[7], (BRANCHES,), SUF // 8, SUF + 1), jax.random.fold_in(key_of[7], 1), SUF // 8, SUF).astype(jnp.int32),
        "branch_prefix": draw_branch_prefix(jax.random.fold_in(key_of[10], 71), 0),
        "prefix_slot": draw_prefix_slot(jax.random.fold_in(key_of[10], 71), 0),
    }


def rounded(values):
    return lax.optimization_barrier(values.astype(jnp.bfloat16)).astype(jnp.float32)


def reference(queries, prefix_keys, prefix_values, suffix_keys, suffix_values, new_keys, new_values, suffix_lengths, branch_prefix, prefix_slot):
    score_scale = 1.0 / (HD ** 0.5)
    positions = jnp.arange(SUF + STEPS, dtype=jnp.int32)
    step_index = jnp.arange(STEPS, dtype=jnp.int32)

    def one_branch(branch_item):
        query_rows, keys_own, values_own, keys_new, values_new, length, prefix = branch_item
        slot_pick = prefix_slot[prefix]
        keys_pre = lax.dynamic_index_in_dim(prefix_keys, slot_pick, 0, keepdims=False).astype(jnp.float32).reshape(TB, KVH, BLK, HD)
        values_pre = lax.dynamic_index_in_dim(prefix_values, slot_pick, 0, keepdims=False).astype(jnp.float32).reshape(TB, KVH, BLK, HD)
        query_wide = query_rows.astype(jnp.float32).reshape(STEPS, KVH, HPK, HD)
        scores = jnp.einsum("tkhd,bkid->bkthi", query_wide, keys_pre) * score_scale
        block_max = jnp.max(scores, axis=-1)
        weight = jnp.exp(scores - block_max[..., None])
        block_total = jnp.sum(weight, axis=-1)
        mixture = jnp.einsum("bkthi,bkid->bkthd", rounded(weight), values_pre)
        block_out = rounded(mixture / block_total[..., None])
        block_lse = block_max + jnp.log(block_total)
        keys_all = jnp.concatenate([keys_own, keys_new], axis=0).astype(jnp.float32)
        values_all = jnp.concatenate([values_own, values_new], axis=0).astype(jnp.float32)
        own_scores = jnp.einsum("tkhd,skd->kths", query_wide, keys_all) * score_scale
        valid = jnp.where(positions[None, :] < SUF, positions[None, :] < length, positions[None, :] - SUF <= step_index[:, None])
        own_scores = jnp.where(valid[None, :, None, :], own_scores, -jnp.inf)
        own_max = jnp.max(own_scores, axis=-1)
        own_weight = jnp.exp(own_scores - own_max[..., None])
        own_total = jnp.sum(own_weight, axis=-1)
        own_out = jnp.einsum("kths,skd->kthd", rounded(own_weight), values_all) / own_total[..., None]
        own_lse = own_max + jnp.log(own_total)
        ceiling = jnp.maximum(jnp.max(block_lse, axis=0), own_lse)
        block_factor = jnp.exp(block_lse - ceiling[None])
        own_factor = jnp.exp(own_lse - ceiling)
        numerator = jnp.sum(block_factor[..., None] * block_out, axis=0) + own_factor[..., None] * own_out
        denominator = jnp.sum(block_factor, axis=0) + own_factor
        result = numerator / denominator[..., None]
        return jnp.transpose(result, (1, 0, 2, 3)).reshape(STEPS, HEADS, HD).astype(jnp.bfloat16)

    return lax.map(one_branch, (queries, suffix_keys, suffix_values, new_keys, new_values, suffix_lengths, branch_prefix))
```

```python
import functools
import math

import jax
import jax.numpy as jnp
from jax import lax
from jax.experimental import pallas as pl
from jax.experimental.pallas import tpu as pltpu
from jax.sharding import PartitionSpec as P

MESH = pl.DeviceIdType.MESH
BF = jnp.bfloat16
F32 = jnp.float32
NT = (((1,), (1,)), ((), ()))
HD = 128
ROWS = 64
SLOTS = 32
TILES = 18
GROUP = 6
DZ_ORDER = (0, 1, 3, 2)
SCALE = math.log2(math.e) / math.sqrt(HD)


def coords():
    shard = lax.axis_index("shard")
    return lax.axis_index("grp"), shard // 8, (shard // 2) % 4, shard % 2


def place(index):
    return index // 8, (index // 2) % 4, index % 2


def at_offset(dz, dy, dc, sign=1):
    z, x, y, c = coords()
    shard = x * 8 + lax.rem(y + sign * dy + 4, 4) * 2 + lax.rem(c + dc, 2)
    return lax.rem(z + sign * dz + 4, 4), shard


def at_x(dx):
    z, x, y, c = coords()
    return z, lax.rem(x + dx + 4, 4) * 8 + y * 2 + c


def eye_mask(rows):
    shape = (rows, 128)
    return lax.broadcasted_iota(jnp.int32, shape, 0) == lax.broadcasted_iota(jnp.int32, shape, 1)


def to_row(column):
    return jnp.sum(jnp.where(eye_mask(column.shape[0]), column, 0.0), axis=0, keepdims=True)


def to_column(row):
    spread = jnp.where(eye_mask(ROWS), jnp.broadcast_to(row, (ROWS, 128)), 0.0)
    return jnp.sum(spread, axis=1, keepdims=True)


def merge(parts):
    top = functools.reduce(jnp.maximum, [lse for _, lse in parts])
    weights = [jnp.exp2(lse - top) for _, lse in parts]
    total = functools.reduce(jnp.add, weights)
    mixed = functools.reduce(jnp.add, [w * out for w, (out, _) in zip(weights, parts)])
    return mixed / total, top + jnp.log2(total)


def order_places(meta_ref, order_v, order_s, sem):
    column = meta_ref[...].reshape(SLOTS, 128)
    lane = lax.broadcasted_iota(jnp.int32, (SLOTS, 128), 1)
    line = lax.broadcasted_iota(jnp.int32, (SLOTS, 128), 0)
    row = jnp.sum(jnp.where(lane == line, column, 0), axis=0, keepdims=True)
    before = (column == row) & (lane < line)
    rank = jnp.sum(jnp.where(before, 1, 0), axis=1, keepdims=True)
    lane_row = lax.broadcasted_iota(jnp.int32, (1, 128), 1)
    start = jnp.zeros((1, 1), jnp.int32)
    position = rank
    tile_slot = jnp.zeros((1, 128), jnp.int32)
    for slot in range(4):
        position = position + jnp.where(column[:, :1] == slot, start, 0)
        count = jnp.sum(jnp.where((row == slot) & (lane_row < SLOTS), 1, 0), axis=1, keepdims=True)
        start = start + ((count + 1) & -2)
        if slot < 3:
            tile_slot = tile_slot + jnp.where(2 * lane_row >= start, 1, 0)
    position = jnp.broadcast_to(position, (SLOTS, 128))
    order_v[0:1] = jnp.sum(jnp.where(position == lane, line, 0), axis=0, keepdims=True)
    order_v[1:2] = jnp.sum(jnp.where(lane == line, position, 0), axis=0, keepdims=True)
    order_v[2:3] = tile_slot
    copy = pltpu.make_async_copy(order_v, order_s, sem)
    copy.start()
    copy.wait()


def read_order(order_s, line, index):
    return jnp.clip(order_s[line, index], 0, (SLOTS - 1, 2 * TILES - 1, 3)[line])


def attend_chunk(q_ref, order_s, keys_t, values_a, out_ref, lse_ref):
    def step(turn, carry):
        scores = []
        for unit in range(GROUP):
            tile = turn * GROUP + unit
            first = q_ref[read_order(order_s, 0, 2 * tile)]
            second = q_ref[read_order(order_s, 0, 2 * tile + 1)]
            rows = jnp.concatenate([first, second], axis=0)
            keys = keys_t[read_order(order_s, 2, tile)]
            scores.append(jnp.dot(rows, keys, preferred_element_type=F32))
        for unit in range(GROUP):
            tile = turn * GROUP + unit
            top = jnp.max(scores[unit], axis=1, keepdims=True)
            weight = jnp.exp2((scores[unit] - top) * SCALE).astype(BF)
            both = jnp.dot(weight, values_a[read_order(order_s, 2, tile)], preferred_element_type=F32)
            total = both[:, HD:]
            out = (both[:, :HD] / total).astype(BF)
            lse = top * SCALE + jnp.log2(total)
            out_ref[2 * tile] = out[:ROWS]
            out_ref[2 * tile + 1] = out[ROWS:]
            lse_ref[2 * tile] = lse[:ROWS]
            lse_ref[2 * tile + 1] = lse[ROWS:]
        return carry

    lax.fori_loop(0, TILES // GROUP, step, 0)


def spread_heads(src_ref, new_ref, branch, wide, wide_new):
    def step(turn, carry):
        part = src_ref[branch, pl.ds(turn * 64, 64)].astype(F32)
        wide[pl.ds(pl.multiple_of(turn * 512, 512), 512)] = part.reshape(512, HD)
        return carry

    lax.fori_loop(0, 8, step, 0)
    wide_new[0:32] = new_ref[branch].astype(F32).reshape(32, HD)


def own_branch(branch, b, length):
    sk, sv, nk, nv = b["sk_v"], b["sv_v"], b["nk_v"], b["nv_v"]
    spread_heads(sk, nk, branch, b["wide_k"], b["wide_nk"])
    spread_heads(sv, nv, branch, b["wide_v"], b["wide_nv"])
    pad = jnp.zeros((124, HD), F32)

    def step(turn, carry):
        pieces = []
        for unit in range(2):
            head = turn * 2 + unit
            keys = jnp.concatenate(
                [b["wide_k"][pl.ds(head, 512, stride=8)], b["wide_nk"][pl.ds(head, 4, stride=8)], pad], axis=0
            ).astype(BF)
            values = jnp.concatenate(
                [b["wide_v"][pl.ds(head, 512, stride=8)], b["wide_nv"][pl.ds(head, 4, stride=8)], pad], axis=0
            ).astype(BF)
            start = pl.multiple_of(head * 16, 16)
            rows = b["q_v"][branch, :, pl.ds(start, 16), :].reshape(ROWS, HD)
            scores = lax.dot_general(rows, keys, NT, preferred_element_type=F32)
            lane = lax.broadcasted_iota(jnp.int32, scores.shape, 1)
            stage = lax.broadcasted_iota(jnp.int32, scores.shape, 0) // 16
            live = (lane < length) | ((lane >= 512) & (lane - 512 <= stage))
            pieces.append((jnp.where(live, scores, -jnp.inf), values))
        for unit in range(2):
            head = turn * 2 + unit
            scores, values = pieces[unit]
            top = jnp.max(scores, axis=1, keepdims=True)
            weight = jnp.exp2((scores - top) * SCALE)
            total = jnp.sum(weight, axis=1, keepdims=True)
            mixed = jnp.dot(weight.astype(BF), values, preferred_element_type=F32)
            b["own_o"][branch, head] = mixed / total
            b["own_l"][branch, head] = jnp.broadcast_to(top * SCALE + jnp.log2(total), (ROWS, 128))
        return carry

    lax.fori_loop(0, 4, step, 0)


def pick_rows(order_s, out_ref, lse_ref, index):
    where = read_order(order_s, 1, index)
    return out_ref[where], lse_ref[where]


def kernel(prefix_ref, slot_ref, length_ref, q_hbm, pk_hbm, pv_hbm, sk_hbm, sv_hbm, nk_hbm, nv_hbm, o_ref, *scratch):
    b = dict(zip(NAMES, scratch))
    z, x, y, c = coords()

    def local(index, src, dst):
        copy = pltpu.make_async_copy(src, dst, b["local_sem"].at[index])
        copy.start()
        return copy

    load_q = local(0, q_hbm, b["q_v"])
    load_k = local(1, pk_hbm, b["pk_v"])
    load_v = local(2, pv_hbm, b["va"].at[:, :, pl.ds(0, HD)])
    load_own = [
        local(3, sk_hbm, b["sk_v"]),
        local(4, sv_hbm, b["sv_v"]),
        local(5, nk_hbm, b["nk_v"]),
        local(6, nv_hbm, b["nv_v"]),
    ]

    barrier = pltpu.get_barrier_semaphore()
    for index in range(1, SLOTS):
        pl.semaphore_signal(barrier, inc=1, device_id=at_offset(*place(index)), device_id_type=MESH)
    for dx in (1, -1):
        pl.semaphore_signal(barrier, inc=1, device_id=at_x(dx), device_id_type=MESH)

    slots = [slot_ref[prefix_ref[i]] for i in range(2)]
    groups = [s // 4 for s in slots]

    def remote(src, dst, send, recv, device):
        return pltpu.make_async_remote_copy(
            src_ref=src, dst_ref=dst, send_sem=send, recv_sem=recv, device_id=device, device_id_type=MESH
        )

    def q_copies(index):
        device = at_offset(*place(index))
        return (
            remote(b["sb"].at[index], b["qx0"].at[index], b["q_send"].at[index], b["q_recv"].at[index], device),
            remote(b["mb"].at[index // 8], b["mx0"].at[index], b["m_send"].at[index], b["m_recv"].at[index], device),
        )

    load_q.wait()
    started = False
    for dz in DZ_ORDER:
        group = lax.rem(z + dz, 4)
        second = (groups[1] == group).astype(jnp.int32)
        local_slot = jnp.where(groups[1] == group, slots[1], slots[0]) % 4
        b["mb"][dz] = jnp.full((1, 128), local_slot, jnp.int32)
        for low in range(8):
            index = dz * 8 + low
            _, dy, dc = place(index)
            head = lax.rem(y + dy, 4) * 2 + lax.rem(c + dc, 2)
            rows = b["q_v"][second, :, pl.ds(pl.multiple_of(head * 16, 16), 16), :].reshape(ROWS, HD)
            if index == 0:
                b["qx0"][0] = rows
                b["mx0"][0] = b["mb"][0]
            else:
                b["sb"][index] = rows
        if not started:
            pl.semaphore_wait(barrier, SLOTS - 1 + 2)
            started = True
        for low in range(8):
            index = dz * 8 + low
            if index:
                for copy in q_copies(index):
                    copy.start()

    def x_copies(dz, side):
        part = pl.ds(dz * 8, 8)
        target = b["qx1"] if side == 0 else b["qx2"]
        mtarget = b["mx1"] if side == 0 else b["mx2"]
        device = at_x(1 if side == 0 else -1)
        return (
            remote(b["qx0"].at[part], target.at[part], b["x_send"].at[side, dz], b["x_recv"].at[side, dz], device),
            remote(b["mx0"].at[part], mtarget.at[part], b["xm_send"].at[side, dz], b["xm_recv"].at[side, dz], device),
        )

    def f_copies(dz, side):
        part = pl.ds(dz * 8 + side * 4, 4)
        source = b["qx1"] if side == 0 else b["qx2"]
        msource = b["mx1"] if side == 0 else b["mx2"]
        device = at_x(1 if side == 0 else -1)
        return (
            remote(source.at[part], b["qx3"].at[part], b["f_send"].at[side, dz], b["f_recv"].at[side, dz], device),
            remote(msource.at[part], b["mx3"].at[part], b["fm_send"].at[side, dz], b["fm_recv"].at[side, dz], device),
        )

    def pass_x(dz):
        for low in range(8):
            index = dz * 8 + low
            if index:
                for copy in q_copies(index):
                    copy.wait_recv()
        for side in range(2):
            for copy in x_copies(dz, side):
                copy.start()

    def pass_on(dz):
        for side in range(2):
            for copy in x_copies(dz, side):
                copy.wait_recv()
            for copy in f_copies(dz, side):
                copy.start()

    for slot in range(4):
        b["va"][slot, :, HD:] = jnp.ones((1024, HD), BF)
    load_k.wait()
    for slot in range(4):
        b["kt"][slot] = b["pk_v"][slot].T
    pass_x(0)
    for copy in load_own:
        copy.wait()
    own_branch(0, b, length_ref[0])
    pass_x(1)
    pass_x(3)
    own_branch(1, b, length_ref[1])
    pass_x(2)
    load_v.wait()

    def chunk(number):
        order_places(b["mx%d" % number], b["order_v"], b["order%d" % number], b["local_sem"].at[7])
        attend_chunk(
            b["qx%d" % number], b["order%d" % number], b["kt"], b["va"], b["ot%d" % number], b["lt%d" % number]
        )

    def part_of(number, index):
        return pick_rows(b["order%d" % number], b["ot%d" % number], b["lt%d" % number], index)

    chunk(0)
    for dz in (0, 1, 3):
        pass_on(dz)
    pass_on(2)

    def a_copies(side):
        device = at_x(-1 if side == 0 else 1)
        return (
            remote(b["a_out"].at[side], b["a_in"].at[side], b["a_send"].at[side], b["a_recv"].at[side], device),
            remote(b["al_out"].at[side], b["al_in"].at[side], b["al_send"].at[side], b["al_recv"].at[side], device),
        )

    def c_copies(side, dz):
        device = at_x(-1 if side == 0 else 1)
        part = pl.ds(dz * 4, 4)
        lpart = pl.ds(dz * 8, 8)
        return (
            remote(
                b["c_out"].at[side, part], b["c_in"].at[side, part], b["c_send"].at[side, dz], b["c_recv"].at[side, dz], device
            ),
            remote(
                b["cl_out"].at[side, lpart], b["cl_in"].at[side, lpart], b["cl_send"].at[side, dz], b["cl_recv"].at[side, dz],
                device,
            ),
        )

    def b_copies(side, dz):
        device = at_x(-1 if side == 0 else 1)
        part = pl.ds(dz * 4, 4)
        lpart = pl.ds(dz * 8, 8)
        return (
            remote(
                b["b_out"].at[side, part], b["b_in"].at[side, part], b["b_send"].at[side, dz], b["b_recv"].at[side, dz], device
            ),
            remote(
                b["bl_out"].at[side, lpart], b["bl_in"].at[side, lpart], b["bl_send"].at[side, dz], b["bl_recv"].at[side, dz],
                device,
            ),
        )

    def send_plain(number, side, half, out, lse, dz_list, copies):
        for dz in dz_list:
            def step(low, carry):
                rows, column = part_of(number, dz * 8 + half * 4 + low)
                out[side, dz * 4 + low] = rows
                lse[side, pl.ds(dz * 8 + low, 1)] = to_row(column)
                return carry

            lax.fori_loop(0, 4, step, 0)
            for copy in copies(dz):
                copy.start()

    chunk(1)
    send_plain(1, 0, 1, b["a_out"], b["al_out"], range(4), lambda dz: a_copies(0) if dz == 3 else ())
    chunk(2)
    send_plain(2, 1, 0, b["a_out"], b["al_out"], range(4), lambda dz: a_copies(1) if dz == 3 else ())
    for dz in DZ_ORDER:
        for side in range(2):
            for copy in f_copies(dz, side):
                copy.wait_recv()
    chunk(3)
    for dz in DZ_ORDER:
        for side in range(2):
            send_plain(3, side, side, b["c_out"], b["cl_out"], [dz], functools.partial(c_copies, side))

    for dz in DZ_ORDER:
        for side in range(2):
            for copy in c_copies(side, dz):
                copy.wait_recv()

            def step(low, carry):
                rows, column = part_of(1 + side, dz * 8 + side * 4 + low)
                far = to_column(b["cl_in"][side, pl.ds(dz * 8 + low, 1)])
                out, lse = merge([(rows.astype(F32), column), (b["c_in"][side, dz * 4 + low].astype(F32), far)])
                b["b_out"][side, dz * 4 + low] = out.astype(BF)
                b["bl_out"][side, pl.ds(dz * 8 + low, 1)] = to_row(lse)
                return carry

            lax.fori_loop(0, 4, step, 0)
            for copy in b_copies(side, dz):
                copy.start()

    def h_copies(index):
        device = at_offset(*place(index), sign=-1)
        return (
            remote(b["h_out"].at[index], b["h_in"].at[index], b["h_send"].at[index], b["h_recv"].at[index], device),
            remote(b["hl_out"].at[index], b["hl_in"].at[index], b["hl_send"].at[index], b["hl_recv"].at[index], device),
        )

    for side in range(2):
        for copy in a_copies(side):
            copy.wait_recv()
    for dz in DZ_ORDER:
        for half in range(2):
            for copy in b_copies(half, dz):
                copy.wait_recv()

            def step(low, carry):
                index = dz * 8 + half * 4 + low
                rows, column = part_of(0, index)
                plain = to_column(b["al_in"][1 - half, pl.ds(dz * 8 + low, 1)])
                joined = to_column(b["bl_in"][half, pl.ds(dz * 8 + low, 1)])
                out, lse = merge(
                    [
                        (rows.astype(F32), column),
                        (b["a_in"][1 - half, dz * 4 + low].astype(F32), plain),
                        (b["b_in"][half, dz * 4 + low].astype(F32), joined),
                    ]
                )
                b["h_out"][index] = out.astype(BF)
                b["hl_out"][index] = to_row(lse)
                return carry

            lax.fori_loop(0, 4, step, 0)
            for low in range(4):
                index = dz * 8 + half * 4 + low
                if index:
                    for copy in h_copies(index):
                        copy.start()
                else:
                    b["h_in"][0] = b["h_out"][0]
                    b["hl_in"][0] = b["hl_out"][0]

    for index in range(1, SLOTS):
        for copy in h_copies(index):
            copy.wait_recv()

    for branch in range(2):
        away = lax.rem(groups[branch] - z + 4, 4)

        def step(low, carry):
            dy = low // 2
            dc = low % 2
            head = lax.rem(y + dy, 4) * 2 + lax.rem(c + dc, 2)
            from_prefix = b["h_in"][away * 8 + low].astype(F32)
            lse = to_column(b["hl_in"][away * 8 + low])
            out, _ = merge([(from_prefix, lse), (b["own_o"][branch, head], b["own_l"][branch, head])])
            o_ref[branch, :, pl.ds(pl.multiple_of(head * 16, 16), 16), :] = out.astype(BF).reshape(4, 16, HD)
            return carry

        lax.fori_loop(0, 8, step, 0)

    for index in range(1, SLOTS):
        for copy in q_copies(index) + h_copies(index):
            copy.wait_send()
    for side in range(2):
        for copy in a_copies(side):
            copy.wait_send()
        for dz in range(4):
            for copy in x_copies(dz, side) + f_copies(dz, side) + c_copies(side, dz) + b_copies(side, dz):
                copy.wait_send()


def scratch_shapes():
    dma = pltpu.SemaphoreType.DMA
    vmem = pltpu.VMEM
    shapes = {
        "q_v": vmem((2, 4, 128, HD), BF),
        "pk_v": vmem((4, 1024, HD), BF),
        "kt": vmem((4, HD, 1024), BF),
        "va": vmem((4, 1024, 2 * HD), BF),
        "sk_v": vmem((2, 512, 8, HD), BF),
        "sv_v": vmem((2, 512, 8, HD), BF),
        "nk_v": vmem((2, 4, 8, HD), BF),
        "nv_v": vmem((2, 4, 8, HD), BF),
        "wide_k": vmem((4104, HD), F32),
        "wide_v": vmem((4104, HD), F32),
        "wide_nk": vmem((40, HD), F32),
        "wide_nv": vmem((40, HD), F32),
        "own_o": vmem((2, 8, ROWS, HD), F32),
        "own_l": vmem((2, 8, ROWS, HD), F32),
        "sb": vmem((SLOTS, ROWS, HD), BF),
        "mb": vmem((4, 1, 128), jnp.int32),
        "order_v": vmem((8, 128), jnp.int32),
        "a_out": vmem((2, 16, ROWS, HD), BF),
        "a_in": vmem((2, 16, ROWS, HD), BF),
        "c_out": vmem((2, 16, ROWS, HD), BF),
        "c_in": vmem((2, 16, ROWS, HD), BF),
        "b_out": vmem((2, 16, ROWS, HD), BF),
        "b_in": vmem((2, 16, ROWS, HD), BF),
        "h_out": vmem((SLOTS, ROWS, HD), BF),
        "h_in": vmem((SLOTS, ROWS, HD), BF),
        "hl_out": vmem((SLOTS, 1, 128), F32),
        "hl_in": vmem((SLOTS, 1, 128), F32),
        "local_sem": dma((8,)),
    }
    for name in ("al", "cl", "bl"):
        shapes[name + "_out"] = vmem((2, 32, 128), F32)
        shapes[name + "_in"] = vmem((2, 32, 128), F32)
    for number in range(4):
        shapes["qx%d" % number] = vmem((SLOTS, ROWS, HD), BF)
        shapes["mx%d" % number] = vmem((SLOTS, 1, 128), jnp.int32)
        shapes["order%d" % number] = pltpu.SMEM((8, 128), jnp.int32)
        shapes["ot%d" % number] = vmem((2 * TILES, ROWS, HD), BF)
        shapes["lt%d" % number] = vmem((2 * TILES, ROWS, HD), F32)
    for name, count in (
        ("q", (SLOTS,)), ("m", (SLOTS,)), ("x", (2, 4)), ("xm", (2, 4)), ("f", (2, 4)), ("fm", (2, 4)),
        ("a", (2,)), ("al", (2,)), ("c", (2, 4)), ("cl", (2, 4)), ("b", (2, 4)), ("bl", (2, 4)),
        ("h", (SLOTS,)), ("hl", (SLOTS,)),
    ):
        shapes[name + "_send"] = dma(count)
        shapes[name + "_recv"] = dma(count)
    return shapes


NAMES = tuple(scratch_shapes())


def body(
    queries, prefix_keys, prefix_values, suffix_keys, suffix_values, new_keys, new_values, suffix_lengths, branch_prefix,
    prefix_slot,
):
    smem = pl.BlockSpec(memory_space=pltpu.SMEM)
    hbm = pl.BlockSpec(memory_space=pl.ANY)
    return pl.pallas_call(
        kernel,
        out_shape=jax.ShapeDtypeStruct(queries.shape, BF),
        in_specs=[smem] * 3 + [hbm] * 7,
        out_specs=pl.BlockSpec(memory_space=pltpu.VMEM),
        scratch_shapes=list(scratch_shapes().values()),
        compiler_params=pltpu.CompilerParams(collective_id=0, has_side_effects=True, vmem_limit_bytes=60 << 20),
        name="attend",
    )(
        branch_prefix, prefix_slot, suffix_lengths, queries, prefix_keys[:, 0], prefix_values[:, 0], suffix_keys,
        suffix_values, new_keys, new_values,
    )


def solution(mesh):
    both = P(("grp", "shard"), None, None, None)
    prefix = P("grp", "shard", None, None)
    flat = P(("grp", "shard"))
    return jax.shard_map(
        body,
        mesh=mesh,
        in_specs=(both, prefix, prefix, both, both, both, both, flat, flat, P()),
        out_specs=both,
        check_vma=False,
    )
```

```python
import functools
import math

import jax
import jax.numpy as jnp
from jax import lax
from jax.experimental import pallas as pl
from jax.experimental.pallas import tpu as pltpu
from jax.sharding import PartitionSpec as P

MESH = pl.DeviceIdType.MESH
BF = jnp.bfloat16
F32 = jnp.float32
NT = (((1,), (1,)), ((), ()))
HD = 128
ROWS = 64
SLOTS = 32
TILES = 18
GROUP = 6
DZ_ORDER = (0, 1, 3, 2)
BACK_ORDER = (2, 1, 3, 0)
SCALE = math.log2(math.e) / math.sqrt(HD)


def beside(side, dz):
    return (1 if dz < 2 else 2), side * 16 + (8 if dz in (1, 2) else 0)


def coords():
    shard = lax.axis_index("shard")
    return lax.axis_index("grp"), shard // 8, (shard // 2) % 4, shard % 2


def place(index):
    return index // 8, (index // 2) % 4, index % 2


def at_offset(dz, dy, dc, sign=1):
    z, x, y, c = coords()
    shard = x * 8 + lax.rem(y + sign * dy + 4, 4) * 2 + lax.rem(c + dc, 2)
    return lax.rem(z + sign * dz + 4, 4), shard


def at_x(dx):
    z, x, y, c = coords()
    return z, lax.rem(x + dx + 4, 4) * 8 + y * 2 + c


def eye_mask(rows):
    shape = (rows, 128)
    return lax.broadcasted_iota(jnp.int32, shape, 0) == lax.broadcasted_iota(jnp.int32, shape, 1)


def to_row(column):
    return jnp.sum(jnp.where(eye_mask(column.shape[0]), column, 0.0), axis=0, keepdims=True)


def to_column(row):
    spread = jnp.where(eye_mask(ROWS), jnp.broadcast_to(row, (ROWS, 128)), 0.0)
    return jnp.sum(spread, axis=1, keepdims=True)


def merge(parts):
    top = functools.reduce(jnp.maximum, [lse for _, lse in parts])
    weights = [jnp.exp2(lse - top) for _, lse in parts]
    total = functools.reduce(jnp.add, weights)
    mixed = functools.reduce(jnp.add, [w * out for w, (out, _) in zip(weights, parts)])
    return mixed / total, top + jnp.log2(total)


def order_places(meta_refs, source_ref, order_v, order_s, sem):
    for low in range(8):
        for branch in range(2):
            row = 32 + 2 * low + branch
            order_v[row : row + 1] = source_ref[low, branch]
    lane = lax.broadcasted_iota(jnp.int32, (SLOTS, 128), 1)
    line = lax.broadcasted_iota(jnp.int32, (SLOTS, 128), 0)
    lane_row = lax.broadcasted_iota(jnp.int32, (1, 128), 1)
    for number, pieces in enumerate(meta_refs):
        column = jnp.concatenate([ref[dz].reshape(8, 128) for ref, dz in pieces], axis=0)
        row = jnp.sum(jnp.where(lane == line, column, 0), axis=0, keepdims=True)
        before = (column == row) & (lane < line)
        rank = jnp.sum(jnp.where(before, 1, 0), axis=1, keepdims=True)
        start = jnp.zeros((1, 1), jnp.int32)
        position = rank
        tile_slot = jnp.zeros((1, 128), jnp.int32)
        for slot in range(4):
            position = position + jnp.where(column[:, :1] == slot, start, 0)
            count = jnp.sum(jnp.where((row == slot) & (lane_row < SLOTS), 1, 0), axis=1, keepdims=True)
            start = start + ((count + 1) & -2)
            if slot < 3:
                tile_slot = tile_slot + jnp.where(2 * lane_row >= start, 1, 0)
        position = jnp.broadcast_to(position, (SLOTS, 128))
        order_v[8 * number : 8 * number + 1] = jnp.sum(jnp.where(position == lane, line, 0), axis=0, keepdims=True)
        order_v[8 * number + 1 : 8 * number + 2] = jnp.sum(
            jnp.where(lane == line, position, 0), axis=0, keepdims=True
        )
        order_v[8 * number + 2 : 8 * number + 3] = tile_slot
    copy = pltpu.make_async_copy(order_v, order_s, sem)
    copy.start()
    copy.wait()


def read_order(order, line, index):
    order_s, number = order
    return jnp.clip(order_s[8 * number + line, index], 0, (SLOTS - 1, 2 * TILES - 1, 3)[line])


def attend_chunk(q_ref, order_s, keys_t, values_a, out_ref, lse_ref):
    def step(turn, carry):
        scores = []
        for unit in range(GROUP):
            tile = turn * GROUP + unit
            first = q_ref[read_order(order_s, 0, 2 * tile)]
            second = q_ref[read_order(order_s, 0, 2 * tile + 1)]
            rows = jnp.concatenate([first, second], axis=0)
            keys = keys_t[read_order(order_s, 2, tile)]
            scores.append(jnp.dot(rows, keys, preferred_element_type=F32))
        for unit in range(GROUP):
            tile = turn * GROUP + unit
            top = jnp.max(scores[unit], axis=1, keepdims=True)
            weight = jnp.exp2((scores[unit] - top) * SCALE).astype(BF)
            both = jnp.dot(weight, values_a[read_order(order_s, 2, tile)], preferred_element_type=F32)
            total = both[:, HD:]
            out = (both[:, :HD] / total).astype(BF)
            lse = top * SCALE + jnp.log2(total)
            out_ref[2 * tile] = out[:ROWS]
            out_ref[2 * tile + 1] = out[ROWS:]
            lse_ref[2 * tile] = lse[:ROWS]
            lse_ref[2 * tile + 1] = lse[ROWS:]
        return carry

    lax.fori_loop(0, TILES // GROUP, step, 0)


def spread_heads(src_ref, new_ref, branch, wide, wide_new):
    def step(turn, carry):
        part = src_ref[branch, pl.ds(turn * 64, 64)].astype(F32)
        wide[pl.ds(pl.multiple_of(turn * 512, 512), 512)] = part.reshape(512, HD)
        return carry

    lax.fori_loop(0, 8, step, 0)
    wide_new[0:32] = new_ref[branch].astype(F32).reshape(32, HD)


def own_spread(branch, b):
    sk, sv, nk, nv = b["sk_v"], b["sv_v"], b["nk_v"], b["nv_v"]
    spread_heads(sk, nk, branch, b["wide_k"], b["wide_nk"])
    spread_heads(sv, nv, branch, b["wide_v"], b["wide_nv"])


def own_heads(branch, b, length, turns):
    pad = jnp.zeros((124, HD), F32)

    def step(turn, carry):
        pieces = []
        for unit in range(4):
            head = turn * 4 + unit
            keys = jnp.concatenate(
                [b["wide_k"][pl.ds(head, 512, stride=8)], b["wide_nk"][pl.ds(head, 4, stride=8)], pad], axis=0
            ).astype(BF)
            values = jnp.concatenate(
                [b["wide_v"][pl.ds(head, 512, stride=8)], b["wide_nv"][pl.ds(head, 4, stride=8)], pad], axis=0
            ).astype(BF)
            start = pl.multiple_of(head * 16, 16)
            rows = b["q_v"][branch, :, pl.ds(start, 16), :].reshape(ROWS, HD)
            scores = lax.dot_general(rows, keys, NT, preferred_element_type=F32)
            lane = lax.broadcasted_iota(jnp.int32, scores.shape, 1)
            stage = lax.broadcasted_iota(jnp.int32, scores.shape, 0) // 16
            live = (lane < length) | ((lane >= 512) & (lane - 512 <= stage))
            pieces.append((jnp.where(live, scores, -jnp.inf), values))
        for unit in range(4):
            head = turn * 4 + unit
            scores, values = pieces[unit]
            top = jnp.max(scores, axis=1, keepdims=True)
            weight = jnp.exp2((scores - top) * SCALE)
            total = jnp.sum(weight, axis=1, keepdims=True)
            mixed = jnp.dot(weight.astype(BF), values, preferred_element_type=F32)
            b["own_o"][branch, head] = mixed / total
            b["own_l"][branch, head] = jnp.broadcast_to(top * SCALE + jnp.log2(total), (ROWS, 128))
        return carry

    lax.fori_loop(*turns, step, 0)


def pick_rows(order_s, out_ref, lse_ref, index):
    where = read_order(order_s, 1, index)
    return out_ref[where], lse_ref[where]


def kernel(prefix_ref, slot_ref, length_ref, q_hbm, pk_hbm, pv_hbm, sk_hbm, sv_hbm, nk_hbm, nv_hbm, o_ref, *scratch):
    b = dict(zip(NAMES, scratch))
    z, x, y, c = coords()

    def local(index, src, dst):
        copy = pltpu.make_async_copy(src, dst, b["local_sem"].at[index])
        copy.start()
        return copy

    load_q = local(0, q_hbm, b["q_v"])
    load_k = local(1, pk_hbm, b["pk_v"])
    load_v = local(2, pv_hbm, b["va"].at[:, :, pl.ds(0, HD)])
    load_own = [
        local(3, sk_hbm, b["sk_v"]),
        local(4, sv_hbm, b["sv_v"]),
        local(5, nk_hbm, b["nk_v"]),
        local(6, nv_hbm, b["nv_v"]),
    ]

    barrier = pltpu.get_barrier_semaphore()
    partners = [at_offset(0, *place(low)[1:]) for low in range(1, 8)]
    partners += [at_offset(dz, 0, 0) for dz in range(1, 4)] + [at_x(1), at_x(-1)]
    for partner in partners:
        pl.semaphore_signal(barrier, inc=1, device_id=partner, device_id_type=MESH)

    slots = [slot_ref[prefix_ref[i]] for i in range(2)]
    groups = [s // 4 for s in slots]

    def remote(src, dst, send, recv, device):
        return pltpu.make_async_remote_copy(
            src_ref=src, dst_ref=dst, send_sem=send, recv_sem=recv, device_id=device, device_id_type=MESH
        )

    def pair(name, key, src, dst, device):
        return remote(src, dst, b[name + "_send"].at[key], b[name + "_recv"].at[key], device)

    def qy_copy(low):
        _, dy, dc = place(low)
        head = lax.rem(y + dy, 4) * 2 + lax.rem(c + dc, 2)
        rows = pl.ds(pl.multiple_of(head * 16, 16), 16)
        return pair("qy", low, b["q_v"].at[:, :, rows, :], b["qy"].at[low], at_offset(0, dy, dc))

    def my_copy(low):
        return pair("my", low, b["mb"], b["my"].at[low], at_offset(0, *place(low)[1:]))

    def qz_copy(dz):
        return pair("qz", dz, b["zb"].at[dz], b["qx0"].at[pl.ds(dz * 8, 8)], at_offset(dz, 0, 0))

    def mz_copy(dz):
        return pair("mz", dz, b["mz"].at[dz], b["mx0"].at[dz], at_offset(dz, 0, 0))

    for branch in range(2):
        b["mb"][branch] = jnp.full((1, 128), slots[branch], jnp.int32)
    pl.semaphore_wait(barrier, len(partners))
    for low in range(1, 8):
        my_copy(low).start()
    load_q.wait()
    for low in range(1, 8):
        qy_copy(low).start()
    head = y * 2 + c
    b["qy"][0] = b["q_v"][:, :, pl.ds(pl.multiple_of(head * 16, 16), 16), :]
    b["my"][0] = b["mb"][...]

    def build_meta(dz):
        group = lax.rem(z + dz, 4)
        for low in range(8):
            first, second = b["my"][low, 0], b["my"][low, 1]
            b["mz" if dz else "mx0"][dz, low] = jnp.where((second // 4) == group, second, first) % 4

    def build(dz):
        group = lax.rem(z + dz, 4)
        target = b["zb"] if dz else b["qx0"]
        for low in range(8):
            pick = (b["my"][low, 1] // 4) == group
            pick_rows = jnp.broadcast_to(pick, (ROWS, HD))
            rows = [b["qy"][low, branch].reshape(ROWS, HD).astype(F32) for branch in range(2)]
            chosen = jnp.where(pick_rows, rows[1], rows[0]).astype(BF)
            if dz == 0:
                target[low] = chosen
            else:
                target[dz, low] = chosen

    def x_copy(dz, side):
        batch, base = beside(side, dz)
        source = b["qx0"].at[pl.ds(dz * 8, 8)]
        return pair("x", (side, dz), source, b["qx%d" % batch].at[pl.ds(base, 8)], at_x(1 - 2 * side))

    def xm_copy(side):
        return pair("xm", side, b["mx0"], b["mx%d" % (1 + side)], at_x(1 - 2 * side))

    def f_copy(dz, side):
        batch, base = beside(side, dz)
        source = b["qx%d" % batch].at[pl.ds(base + side * 4, 4)]
        return pair("f", (side, dz), source, b["qx3"].at[pl.ds(dz * 8 + side * 4, 4)], at_x(1 - 2 * side))

    def fm_copy():
        return pair("fm", 0, b["mx1"], b["mx3"], at_x(1))

    def pass_x(dz):
        if dz:
            qz_copy(dz).wait_recv()
        for side in range(2):
            x_copy(dz, side).start()

    def pass_on(dz):
        for side in range(2):
            x_copy(dz, side).wait_recv()
            f_copy(dz, side).start()

    for slot in range(4):
        b["va"][slot, :, HD:] = jnp.ones((1024, HD), BF)
    load_k.wait()
    for slot in range(4):
        b["kt"][slot] = b["pk_v"][slot].T
    for low in range(1, 8):
        my_copy(low).wait_recv()
    for dz in range(4):
        build_meta(dz)
        if dz:
            mz_copy(dz).start()
    for low in range(1, 8):
        qy_copy(low).wait_recv()
    build(0)
    pass_x(0)
    for dz in (1, 3):
        build(dz)
        qz_copy(dz).start()
    for copy in load_own:
        copy.wait()
    own_spread(0, b)
    build(2)
    for dz in range(1, 4):
        mz_copy(dz).wait_recv()
    for side in range(2):
        xm_copy(side).start()
    qz_copy(2).start()
    own_heads(0, b, length_ref[0], (0, 2))
    for side in range(2):
        xm_copy(side).wait_recv()
    fm_copy().start()
    pass_x(1)
    pass_x(3)
    own_spread(1, b)
    own_heads(1, b, length_ref[1], (0, 2))
    fm_copy().wait_recv()
    order_places(
        [
            [(b["mx0"], dz) for dz in range(4)],
            [(b["mx%d" % (1 + side)], dz) for side in range(2) for dz in (0, 1)],
            [(b["mx%d" % (1 + side)], dz) for side in range(2) for dz in (3, 2)],
            [(b["mx3"], dz) for dz in range(4)],
        ],
        b["my"], b["order_v"], b["order_s"], b["local_sem"].at[7],
    )
    load_v.wait()
    pass_x(2)
    pass_on(0)

    def chunk(number):
        attend_chunk(
            b["qx%d" % number], (b["order_s"], number), b["kt"], b["va"], b["ot%d" % number], b["lt%d" % number]
        )

    def part_of(number, index):
        return pick_rows((b["order_s"], number), b["ot%d" % number], b["lt%d" % number], index)

    chunk(0)
    pass_on(1)

    def a_copies(side, late):
        device = at_x(-1 if side == 0 else 1)
        part = pl.ds(late * 8, 8)
        lpart = pl.ds(late * 16, 16)
        return (
            pair("a", (side, late), b["a_out"].at[side, part], b["a_in"].at[side, part], device),
            pair("al", (side, late), b["al_out"].at[side, lpart], b["al_in"].at[side, lpart], device),
        )

    def c_copies(side, dz):
        device = at_x(-1 if side == 0 else 1)
        part = pl.ds(dz * 4, 4)
        lpart = pl.ds(dz * 8, 8)
        return (
            remote(
                b["c_out"].at[side, part], b["c_in"].at[side, part], b["c_send"].at[side, dz], b["c_recv"].at[side, dz], device
            ),
            remote(
                b["cl_out"].at[side, lpart], b["cl_in"].at[side, lpart], b["cl_send"].at[side, dz], b["cl_recv"].at[side, dz],
                device,
            ),
        )

    def b_copies(side, dz):
        device = at_x(-1 if side == 0 else 1)
        part = pl.ds(dz * 4, 4)
        lpart = pl.ds(dz * 8, 8)
        return (
            remote(
                b["b_out"].at[side, part], b["b_in"].at[side, part], b["b_send"].at[side, dz], b["b_recv"].at[side, dz], device
            ),
            remote(
                b["bl_out"].at[side, lpart], b["bl_in"].at[side, lpart], b["bl_send"].at[side, dz], b["bl_recv"].at[side, dz],
                device,
            ),
        )

    def put_plain(number, base, out, lse, side, dz):
        def step(low, carry):
            rows, column = part_of(number, base + low)
            out[side, dz * 4 + low] = rows
            lse[side, pl.ds(dz * 8 + low, 1)] = to_row(column)
            return carry

        lax.fori_loop(0, 4, step, 0, unroll=4)

    for late in range(2):
        chunk(1 + late)
        for side in range(2):
            for dz in (2 * late, 2 * late + 1):
                batch, base = beside(side, dz)
                put_plain(batch, base + 4 - 4 * side, b["a_out"], b["al_out"], side, dz)
            for copy in a_copies(side, late):
                copy.start()
        if not late:
            pass_on(3)
            pass_on(2)
    for dz in DZ_ORDER:
        for side in range(2):
            f_copy(dz, side).wait_recv()
    chunk(3)
    for dz in BACK_ORDER:
        for side in range(2):
            put_plain(3, dz * 8 + side * 4, b["c_out"], b["cl_out"], side, dz)
            for copy in c_copies(side, dz):
                copy.start()

    for dz in BACK_ORDER:
        for side in range(2):
            for copy in c_copies(side, dz):
                copy.wait_recv()

            def step(low, carry):
                batch, base = beside(side, dz)
                rows, column = part_of(batch, base + side * 4 + low)
                far = to_column(b["cl_in"][side, pl.ds(dz * 8 + low, 1)])
                out, lse = merge([(rows.astype(F32), column), (b["c_in"][side, dz * 4 + low].astype(F32), far)])
                b["b_out"][side, dz * 4 + low] = out.astype(BF)
                b["bl_out"][side, pl.ds(dz * 8 + low, 1)] = to_row(lse)
                return carry

            lax.fori_loop(0, 4, step, 0, unroll=4)
            for copy in b_copies(side, dz):
                copy.start()

    def hz_copy(dz):
        part = pl.ds(dz * 8, 8)
        return pair("hz", dz, b["h_out"].at[part], b["h_in"].at[part], at_offset(dz, 0, 0, sign=-1))

    def lz_copy(dz):
        return pair("lz", dz, b["l_out"].at[dz], b["l_in"].at[dz], at_offset(dz, 0, 0, sign=-1))

    def hy_copy(low):
        return pair("hy", low, b["yb"].at[low], b["home"].at[low], at_offset(0, *place(low)[1:], sign=-1))

    def ly_copy(low):
        return pair("ly", low, b["lyb"].at[low], b["lhome"].at[low], at_offset(0, *place(low)[1:], sign=-1))

    for side in range(2):
        for copy in a_copies(side, 0) + a_copies(side, 1):
            copy.wait_recv()
    for dz in BACK_ORDER:
        for half in range(2):
            for copy in b_copies(half, dz):
                copy.wait_recv()

            def step(low, carry):
                index = dz * 8 + half * 4 + low
                rows, column = part_of(0, index)
                plain = to_column(b["al_in"][1 - half, pl.ds(dz * 8 + low, 1)])
                joined = to_column(b["bl_in"][half, pl.ds(dz * 8 + low, 1)])
                out, lse = merge(
                    [
                        (rows.astype(F32), column),
                        (b["a_in"][1 - half, dz * 4 + low].astype(F32), plain),
                        (b["b_in"][half, dz * 4 + low].astype(F32), joined),
                    ]
                )
                b["h_out" if dz else "h_in"][index] = out.astype(BF)
                b["l_out" if dz else "l_in"][dz, half * 4 + low] = to_row(lse)
                return carry

            lax.fori_loop(0, 4, step, 0, unroll=4)
        if dz:
            hz_copy(dz).start()
            lz_copy(dz).start()
    for dz in range(1, 4):
        hz_copy(dz).wait_recv()
        lz_copy(dz).wait_recv()
    for low in (4, 5, 6, 7, 2, 3, 1, 0):
        target, ltarget = ("yb", "lyb") if low else ("home", "lhome")
        for branch in range(2):
            slot = jnp.clip(b["order_s"][32 + 2 * low + branch, 0], 0, 15)
            away = lax.rem(slot // 4 - z + 4, 4)
            b[target][low, branch] = b["h_in"][away * 8 + low]
            b[ltarget][low, branch] = b["l_in"][away, low]
        if low:
            hy_copy(low).start()
            ly_copy(low).start()
    for low in range(1, 8):
        hy_copy(low).wait_recv()
        ly_copy(low).wait_recv()

    for branch in range(2):
        def step(low, carry):
            dy = low // 2
            dc = low % 2
            head = lax.rem(y + dy, 4) * 2 + lax.rem(c + dc, 2)
            lse = to_column(b["lhome"][low, branch])
            out, _ = merge(
                [(b["home"][low, branch].astype(F32), lse), (b["own_o"][branch, head], b["own_l"][branch, head])]
            )
            o_ref[branch, :, pl.ds(pl.multiple_of(head * 16, 16), 16), :] = out.astype(BF).reshape(4, 16, HD)
            return carry

        lax.fori_loop(0, 8, step, 0, unroll=4)

    for dz in range(1, 4):
        for copy in (qz_copy, mz_copy, hz_copy, lz_copy):
            copy(dz).wait_send()
    for low in range(1, 8):
        for copy in (qy_copy, my_copy, hy_copy, ly_copy):
            copy(low).wait_send()
    fm_copy().wait_send()
    for side in range(2):
        xm_copy(side).wait_send()
        for copy in a_copies(side, 0) + a_copies(side, 1):
            copy.wait_send()
        for dz in range(4):
            for copy in (x_copy(dz, side), f_copy(dz, side)) + c_copies(side, dz) + b_copies(side, dz):
                copy.wait_send()


def scratch_shapes():
    dma = pltpu.SemaphoreType.DMA
    vmem = pltpu.VMEM
    shapes = {
        "q_v": vmem((2, 4, 128, HD), BF),
        "pk_v": vmem((4, 1024, HD), BF),
        "kt": vmem((4, HD, 1024), BF),
        "va": vmem((4, 1024, 2 * HD), BF),
        "sk_v": vmem((2, 512, 8, HD), BF),
        "sv_v": vmem((2, 512, 8, HD), BF),
        "nk_v": vmem((2, 4, 8, HD), BF),
        "nv_v": vmem((2, 4, 8, HD), BF),
        "wide_k": vmem((4104, HD), F32),
        "wide_v": vmem((4104, HD), F32),
        "wide_nk": vmem((40, HD), F32),
        "wide_nv": vmem((40, HD), F32),
        "own_o": vmem((2, 8, ROWS, HD), F32),
        "own_l": vmem((2, 8, ROWS, HD), F32),
        "qy": vmem((8, 2, 4, 16, HD), BF),
        "zb": vmem((4, 8, ROWS, HD), BF),
        "mb": vmem((2, 1, 128), jnp.int32),
        "my": vmem((8, 2, 1, 128), jnp.int32),
        "mz": vmem((4, 8, 1, 128), jnp.int32),
        "order_v": vmem((48, 128), jnp.int32),
        "order_s": pltpu.SMEM((48, 128), jnp.int32),
        "l_out": vmem((4, 8, 1, 128), F32),
        "l_in": vmem((4, 8, 1, 128), F32),
        "yb": vmem((8, 2, ROWS, HD), BF),
        "home": vmem((8, 2, ROWS, HD), BF),
        "lyb": vmem((8, 2, 1, 128), F32),
        "lhome": vmem((8, 2, 1, 128), F32),
        "a_out": vmem((2, 16, ROWS, HD), BF),
        "a_in": vmem((2, 16, ROWS, HD), BF),
        "c_out": vmem((2, 16, ROWS, HD), BF),
        "c_in": vmem((2, 16, ROWS, HD), BF),
        "b_out": vmem((2, 16, ROWS, HD), BF),
        "b_in": vmem((2, 16, ROWS, HD), BF),
        "h_out": vmem((SLOTS, ROWS, HD), BF),
        "h_in": vmem((SLOTS, ROWS, HD), BF),
        "local_sem": dma((8,)),
    }
    for name in ("al", "cl", "bl"):
        shapes[name + "_out"] = vmem((2, 32, 128), F32)
        shapes[name + "_in"] = vmem((2, 32, 128), F32)
    for number in range(4):
        shapes["qx%d" % number] = vmem((SLOTS, ROWS, HD), BF)
        shapes["mx%d" % number] = vmem((4, 8, 1, 128), jnp.int32)
        shapes["ot%d" % number] = vmem((2 * TILES, ROWS, HD), BF)
        shapes["lt%d" % number] = vmem((2 * TILES, ROWS, HD), F32)
    for name, count in (
        ("qz", (4,)), ("mz", (4,)), ("qy", (8,)), ("my", (8,)), ("x", (2, 4)), ("xm", (2,)), ("f", (2, 4)),
        ("fm", (1,)), ("a", (2, 2)), ("al", (2, 2)), ("c", (2, 4)), ("cl", (2, 4)), ("b", (2, 4)), ("bl", (2, 4)),
        ("hy", (8,)), ("ly", (8,)), ("hz", (4,)), ("lz", (4,)),
    ):
        shapes[name + "_send"] = dma(count)
        shapes[name + "_recv"] = dma(count)
    return shapes


NAMES = tuple(scratch_shapes())


def body(
    queries, prefix_keys, prefix_values, suffix_keys, suffix_values, new_keys, new_values, suffix_lengths, branch_prefix,
    prefix_slot,
):
    smem = pl.BlockSpec(memory_space=pltpu.SMEM)
    hbm = pl.BlockSpec(memory_space=pl.ANY)
    return pl.pallas_call(
        kernel,
        out_shape=jax.ShapeDtypeStruct(queries.shape, BF),
        in_specs=[smem] * 3 + [hbm] * 7,
        out_specs=pl.BlockSpec(memory_space=pltpu.VMEM),
        scratch_shapes=list(scratch_shapes().values()),
        compiler_params=pltpu.CompilerParams(collective_id=0, has_side_effects=True, vmem_limit_bytes=60 << 20),
        name="attend",
    )(
        branch_prefix, prefix_slot, suffix_lengths, queries, prefix_keys[:, 0], prefix_values[:, 0], suffix_keys,
        suffix_values, new_keys, new_values,
    )


def solution(mesh):
    both = P(("grp", "shard"), None, None, None)
    prefix = P("grp", "shard", None, None)
    flat = P(("grp", "shard"))
    return jax.shard_map(
        body,
        mesh=mesh,
        in_specs=(both, prefix, prefix, both, both, both, both, flat, flat, P()),
        out_specs=both,
        check_vma=False,
    )
```

```python
import functools
import math

import jax
import jax.numpy as jnp
from jax import lax
from jax.experimental import pallas as pl
from jax.experimental.pallas import tpu as pltpu
from jax.sharding import PartitionSpec as P

MESH = pl.DeviceIdType.MESH
BF = jnp.bfloat16
F32 = jnp.float32
NT = (((1,), (1,)), ((), ()))
HD = 128
ROWS = 64
SLOTS = 32
TILES = 18
GROUP = 9
DZ_ORDER = (0, 1, 3, 2)
BACK_ORDER = (2, 1, 3, 0)
SCALE = math.log2(math.e) / math.sqrt(HD)


def beside(side, dz):
    return (1 if dz < 2 else 2), side * 16 + (8 if dz in (1, 2) else 0)


def coords():
    shard = lax.axis_index("shard")
    return lax.axis_index("grp"), shard // 8, (shard // 2) % 4, shard % 2


def place(index):
    return index // 8, (index // 2) % 4, index % 2


def at_offset(dz, dy, dc, sign=1):
    z, x, y, c = coords()
    shard = x * 8 + lax.rem(y + sign * dy + 4, 4) * 2 + lax.rem(c + dc, 2)
    return lax.rem(z + sign * dz + 4, 4), shard


def at_x(dx):
    z, x, y, c = coords()
    return z, lax.rem(x + dx + 4, 4) * 8 + y * 2 + c


def eye_mask(rows):
    shape = (rows, 128)
    return lax.broadcasted_iota(jnp.int32, shape, 0) == lax.broadcasted_iota(jnp.int32, shape, 1)


def to_row(column):
    return jnp.sum(jnp.where(eye_mask(column.shape[0]), column, 0.0), axis=0, keepdims=True)


def to_column(row):
    spread = jnp.where(eye_mask(ROWS), jnp.broadcast_to(row, (ROWS, 128)), 0.0)
    return jnp.sum(spread, axis=1, keepdims=True)


def merge(parts):
    top = functools.reduce(jnp.maximum, [lse for _, lse in parts])
    weights = [jnp.exp2(lse - top) for _, lse in parts]
    total = functools.reduce(jnp.add, weights)
    mixed = functools.reduce(jnp.add, [w * out for w, (out, _) in zip(weights, parts)])
    return mixed / total, top + jnp.log2(total)


def order_places(meta_refs, source_ref, order_v, order_s, sem):
    for low in range(8):
        for branch in range(2):
            row = 32 + 2 * low + branch
            order_v[row : row + 1] = source_ref[low, branch]
    lane = lax.broadcasted_iota(jnp.int32, (SLOTS, 128), 1)
    line = lax.broadcasted_iota(jnp.int32, (SLOTS, 128), 0)
    lane_row = lax.broadcasted_iota(jnp.int32, (1, 128), 1)
    for number, pieces in enumerate(meta_refs):
        column = jnp.concatenate([ref[dz].reshape(8, 128) for ref, dz in pieces], axis=0)
        row = jnp.sum(jnp.where(lane == line, column, 0), axis=0, keepdims=True)
        before = (column == row) & (lane < line)
        rank = jnp.sum(jnp.where(before, 1, 0), axis=1, keepdims=True)
        start = jnp.zeros((1, 1), jnp.int32)
        position = rank
        tile_slot = jnp.zeros((1, 128), jnp.int32)
        for slot in range(4):
            position = position + jnp.where(column[:, :1] == slot, start, 0)
            count = jnp.sum(jnp.where((row == slot) & (lane_row < SLOTS), 1, 0), axis=1, keepdims=True)
            start = start + ((count + 1) & -2)
            if slot < 3:
                tile_slot = tile_slot + jnp.where(2 * lane_row >= start, 1, 0)
        position = jnp.broadcast_to(position, (SLOTS, 128))
        order_v[8 * number : 8 * number + 1] = jnp.sum(jnp.where(position == lane, line, 0), axis=0, keepdims=True)
        order_v[8 * number + 1 : 8 * number + 2] = jnp.sum(
            jnp.where(lane == line, position, 0), axis=0, keepdims=True
        )
        order_v[8 * number + 2 : 8 * number + 3] = tile_slot
    copy = pltpu.make_async_copy(order_v, order_s, sem)
    copy.start()
    copy.wait()


def read_order(order, line, index):
    order_s, number = order
    return jnp.clip(order_s[8 * number + line, index], 0, (SLOTS - 1, 2 * TILES - 1, 3)[line])


def attend_chunk(q_ref, order_s, keys_t, values_a, out_ref, lse_ref):
    def step(turn, carry):
        scores = []
        for unit in range(GROUP):
            tile = turn * GROUP + unit
            first = q_ref[read_order(order_s, 0, 2 * tile)]
            second = q_ref[read_order(order_s, 0, 2 * tile + 1)]
            rows = jnp.concatenate([first, second], axis=0)
            keys = keys_t[read_order(order_s, 2, tile)]
            scores.append(jnp.dot(rows, keys, preferred_element_type=F32))
        for unit in range(GROUP):
            tile = turn * GROUP + unit
            top = jnp.max(scores[unit], axis=1, keepdims=True)
            weight = jnp.exp2((scores[unit] - top) * SCALE).astype(BF)
            both = jnp.dot(weight, values_a[read_order(order_s, 2, tile)], preferred_element_type=F32)
            total = both[:, HD:]
            out = (both[:, :HD] / total).astype(BF)
            lse = top * SCALE + jnp.log2(total)
            out_ref[2 * tile] = out[:ROWS]
            out_ref[2 * tile + 1] = out[ROWS:]
            lse_ref[2 * tile] = lse[:ROWS]
            lse_ref[2 * tile + 1] = lse[ROWS:]
        return carry

    lax.fori_loop(0, TILES // GROUP, step, 0)


def spread_heads(src_ref, new_ref, branch, wide, wide_new):
    def step(turn, carry):
        part = src_ref[branch, pl.ds(turn * 64, 64)].astype(F32)
        wide[pl.ds(pl.multiple_of(turn * 512, 512), 512)] = part.reshape(512, HD)
        return carry

    lax.fori_loop(0, 8, step, 0)
    wide_new[0:32] = new_ref[branch].astype(F32).reshape(32, HD)


def own_spread(branch, b):
    sk, sv, nk, nv = b["sk_v"], b["sv_v"], b["nk_v"], b["nv_v"]
    spread_heads(sk, nk, branch, b["wide_k"], b["wide_nk"])
    spread_heads(sv, nv, branch, b["wide_v"], b["wide_nv"])


def own_heads(branch, b, length, turns):
    pad = jnp.zeros((124, HD), F32)

    def step(turn, carry):
        pieces = []
        for unit in range(4):
            head = turn * 4 + unit
            keys = jnp.concatenate(
                [b["wide_k"][pl.ds(head, 512, stride=8)], b["wide_nk"][pl.ds(head, 4, stride=8)], pad], axis=0
            ).astype(BF)
            values = jnp.concatenate(
                [b["wide_v"][pl.ds(head, 512, stride=8)], b["wide_nv"][pl.ds(head, 4, stride=8)], pad], axis=0
            ).astype(BF)
            start = pl.multiple_of(head * 16, 16)
            rows = b["q_v"][branch, :, pl.ds(start, 16), :].reshape(ROWS, HD)
            scores = lax.dot_general(rows, keys, NT, preferred_element_type=F32)
            lane = lax.broadcasted_iota(jnp.int32, scores.shape, 1)
            stage = lax.broadcasted_iota(jnp.int32, scores.shape, 0) // 16
            live = (lane < length) | ((lane >= 512) & (lane - 512 <= stage))
            pieces.append((jnp.where(live, scores, -jnp.inf), values))
        for unit in range(4):
            head = turn * 4 + unit
            scores, values = pieces[unit]
            top = jnp.max(scores, axis=1, keepdims=True)
            weight = jnp.exp2((scores - top) * SCALE)
            total = jnp.sum(weight, axis=1, keepdims=True)
            mixed = jnp.dot(weight.astype(BF), values, preferred_element_type=F32)
            b["own_o"][branch, head] = mixed / total
            b["own_l"][branch, head] = jnp.broadcast_to(top * SCALE + jnp.log2(total), (ROWS, 128))
        return carry

    lax.fori_loop(*turns, step, 0)


def pick_rows(order_s, out_ref, lse_ref, index):
    where = read_order(order_s, 1, index)
    return out_ref[where], lse_ref[where]


def kernel(prefix_ref, slot_ref, length_ref, q_hbm, pk_hbm, pv_hbm, sk_hbm, sv_hbm, nk_hbm, nv_hbm, o_ref, *scratch):
    b = dict(zip(NAMES, scratch))
    z, x, y, c = coords()

    def local(index, src, dst):
        copy = pltpu.make_async_copy(src, dst, b["local_sem"].at[index])
        copy.start()
        return copy

    load_q = local(0, q_hbm, b["q_v"])
    load_k = local(1, pk_hbm, b["pk_v"])
    load_v = local(2, pv_hbm, b["va"].at[:, :, pl.ds(0, HD)])
    load_own = [
        local(3, sk_hbm, b["sk_v"]),
        local(4, sv_hbm, b["sv_v"]),
        local(5, nk_hbm, b["nk_v"]),
        local(6, nv_hbm, b["nv_v"]),
    ]

    barrier = pltpu.get_barrier_semaphore()
    partners = [at_offset(0, *place(low)[1:]) for low in range(1, 8)]
    partners += [at_offset(dz, 0, 0) for dz in range(1, 4)] + [at_x(1), at_x(-1)]
    for partner in partners:
        pl.semaphore_signal(barrier, inc=1, device_id=partner, device_id_type=MESH)

    slots = [slot_ref[prefix_ref[i]] for i in range(2)]
    groups = [s // 4 for s in slots]

    def remote(src, dst, send, recv, device):
        return pltpu.make_async_remote_copy(
            src_ref=src, dst_ref=dst, send_sem=send, recv_sem=recv, device_id=device, device_id_type=MESH
        )

    def pair(name, key, src, dst, device):
        return remote(src, dst, b[name + "_send"].at[key], b[name + "_recv"].at[key], device)

    def qy_copy(low):
        _, dy, dc = place(low)
        head = lax.rem(y + dy, 4) * 2 + lax.rem(c + dc, 2)
        rows = pl.ds(pl.multiple_of(head * 16, 16), 16)
        return pair("qy", low, b["q_v"].at[:, :, rows, :], b["qy"].at[low], at_offset(0, dy, dc))

    def my_copy(low):
        return pair("my", low, b["mb"], b["my"].at[low], at_offset(0, *place(low)[1:]))

    def qz_copy(dz):
        return pair("qz", dz, b["zb"].at[dz], b["qx0"].at[pl.ds(dz * 8, 8)], at_offset(dz, 0, 0))

    def mz_copy(dz):
        return pair("mz", dz, b["mz"].at[dz], b["mx0"].at[dz], at_offset(dz, 0, 0))

    for branch in range(2):
        b["mb"][branch] = jnp.full((1, 128), slots[branch], jnp.int32)
    pl.semaphore_wait(barrier, len(partners))
    for low in range(1, 8):
        my_copy(low).start()
    load_q.wait()
    for low in (4, 5, 2, 3, 6, 7, 1):
        qy_copy(low).start()
    head = y * 2 + c
    b["qy"][0] = b["q_v"][:, :, pl.ds(pl.multiple_of(head * 16, 16), 16), :]
    b["my"][0] = b["mb"][...]

    def build_meta(dz):
        group = lax.rem(z + dz, 4)
        for low in range(8):
            first, second = b["my"][low, 0], b["my"][low, 1]
            b["mz" if dz else "mx0"][dz, low] = jnp.where((second // 4) == group, second, first) % 4

    def build(dz):
        group = lax.rem(z + dz, 4)
        target = b["zb"] if dz else b["qx0"]
        for low in range(8):
            pick = (b["my"][low, 1] // 4) == group
            pick_rows = jnp.broadcast_to(pick, (ROWS, HD))
            rows = [b["qy"][low, branch].reshape(ROWS, HD).astype(F32) for branch in range(2)]
            chosen = jnp.where(pick_rows, rows[1], rows[0]).astype(BF)
            if dz == 0:
                target[low] = chosen
            else:
                target[dz, low] = chosen

    def x_copy(dz, side):
        batch, base = beside(side, dz)
        source = b["qx0"].at[pl.ds(dz * 8, 8)]
        return pair("x", (side, dz), source, b["qx%d" % batch].at[pl.ds(base, 8)], at_x(1 - 2 * side))

    def xm_copy(side):
        return pair("xm", side, b["mx0"], b["mx%d" % (1 + side)], at_x(1 - 2 * side))

    def f_copy(dz, side):
        batch, base = beside(side, dz)
        source = b["qx%d" % batch].at[pl.ds(base + side * 4, 4)]
        return pair("f", (side, dz), source, b["qx3"].at[pl.ds(dz * 8 + side * 4, 4)], at_x(1 - 2 * side))

    def fm_copy():
        return pair("fm", 0, b["mx1"], b["mx3"], at_x(1))

    def pass_x(dz):
        if dz:
            qz_copy(dz).wait_recv()
        for side in range(2):
            x_copy(dz, side).start()

    def pass_on(dz):
        for side in range(2):
            x_copy(dz, side).wait_recv()
            f_copy(dz, side).start()

    for slot in range(4):
        b["va"][slot, :, HD:] = jnp.ones((1024, HD), BF)
    load_k.wait()
    for slot in range(4):
        b["kt"][slot] = b["pk_v"][slot].T
    for copy in load_own:
        copy.wait()
    own_spread(0, b)
    own_heads(0, b, length_ref[0], (0, 2))
    for low in range(1, 8):
        my_copy(low).wait_recv()
    for dz in range(4):
        build_meta(dz)
        if dz:
            mz_copy(dz).start()
    for low in range(1, 8):
        qy_copy(low).wait_recv()
    build(0)
    pass_x(0)
    for dz in (1, 3):
        build(dz)
        qz_copy(dz).start()
    own_spread(1, b)
    build(2)
    for dz in range(1, 4):
        mz_copy(dz).wait_recv()
    for side in range(2):
        xm_copy(side).start()
    qz_copy(2).start()
    own_heads(1, b, length_ref[1], (0, 2))
    for side in range(2):
        xm_copy(side).wait_recv()
    fm_copy().start()
    pass_x(1)
    pass_x(3)
    fm_copy().wait_recv()
    order_places(
        [
            [(b["mx0"], dz) for dz in range(4)],
            [(b["mx%d" % (1 + side)], dz) for side in range(2) for dz in (0, 1)],
            [(b["mx%d" % (1 + side)], dz) for side in range(2) for dz in (3, 2)],
            [(b["mx3"], dz) for dz in range(4)],
        ],
        b["my"], b["order_v"], b["order_s"], b["local_sem"].at[7],
    )
    load_v.wait()
    pass_x(2)
    pass_on(0)

    def chunk(number):
        attend_chunk(
            b["qx%d" % number], (b["order_s"], number), b["kt"], b["va"], b["ot%d" % number], b["lt%d" % number]
        )

    def part_of(number, index):
        return pick_rows((b["order_s"], number), b["ot%d" % number], b["lt%d" % number], index)

    chunk(0)
    pass_on(1)
    pass_on(3)
    pass_on(2)

    def a_copies(side, late):
        device = at_x(-1 if side == 0 else 1)
        part = pl.ds(late * 8, 8)
        lpart = pl.ds(late * 16, 16)
        return (
            pair("a", (side, late), b["a_out"].at[side, part], b["a_in"].at[side, part], device),
            pair("al", (side, late), b["al_out"].at[side, lpart], b["al_in"].at[side, lpart], device),
        )

    def c_copies(side, dz):
        device = at_x(-1 if side == 0 else 1)
        part = pl.ds(dz * 4, 4)
        lpart = pl.ds(dz * 8, 8)
        return (
            remote(
                b["c_out"].at[side, part], b["c_in"].at[side, part], b["c_send"].at[side, dz], b["c_recv"].at[side, dz], device
            ),
            remote(
                b["cl_out"].at[side, lpart], b["cl_in"].at[side, lpart], b["cl_send"].at[side, dz], b["cl_recv"].at[side, dz],
                device,
            ),
        )

    def b_copies(side, dz):
        device = at_x(-1 if side == 0 else 1)
        part = pl.ds(dz * 4, 4)
        lpart = pl.ds(dz * 8, 8)
        return (
            remote(
                b["b_out"].at[side, part], b["b_in"].at[side, part], b["b_send"].at[side, dz], b["b_recv"].at[side, dz], device
            ),
            remote(
                b["bl_out"].at[side, lpart], b["bl_in"].at[side, lpart], b["bl_send"].at[side, dz], b["bl_recv"].at[side, dz],
                device,
            ),
        )

    def put_plain(number, base, out, lse, side, dz):
        def step(low, carry):
            rows, column = part_of(number, base + low)
            out[side, dz * 4 + low] = rows
            lse[side, pl.ds(dz * 8 + low, 1)] = to_row(column)
            return carry

        lax.fori_loop(0, 4, step, 0, unroll=4)

    def near_chunk(late):
        chunk(1 + late)
        for side in range(2):
            for dz in (2 * late, 2 * late + 1):
                batch, base = beside(side, dz)
                put_plain(batch, base + 4 - 4 * side, b["a_out"], b["al_out"], side, dz)
            for copy in a_copies(side, late):
                copy.start()

    near_chunk(0)
    for dz in DZ_ORDER:
        for side in range(2):
            f_copy(dz, side).wait_recv()
    chunk(3)
    for dz in BACK_ORDER:
        for side in range(2):
            put_plain(3, dz * 8 + side * 4, b["c_out"], b["cl_out"], side, dz)
            for copy in c_copies(side, dz):
                copy.start()
    near_chunk(1)

    for dz in BACK_ORDER:
        for side in range(2):
            for copy in c_copies(side, dz):
                copy.wait_recv()

            def step(low, carry):
                batch, base = beside(side, dz)
                rows, column = part_of(batch, base + side * 4 + low)
                far = to_column(b["cl_in"][side, pl.ds(dz * 8 + low, 1)])
                out, lse = merge([(rows.astype(F32), column), (b["c_in"][side, dz * 4 + low].astype(F32), far)])
                b["b_out"][side, dz * 4 + low] = out.astype(BF)
                b["bl_out"][side, pl.ds(dz * 8 + low, 1)] = to_row(lse)
                return carry

            lax.fori_loop(0, 4, step, 0, unroll=4)
            for copy in b_copies(side, dz):
                copy.start()

    def hz_copy(dz):
        part = pl.ds(dz * 8, 8)
        return pair("hz", dz, b["h_out"].at[part], b["h_in"].at[part], at_offset(dz, 0, 0, sign=-1))

    def lz_copy(dz):
        return pair("lz", dz, b["l_out"].at[dz], b["l_in"].at[dz], at_offset(dz, 0, 0, sign=-1))

    def hy_copy(low):
        return pair("hy", low, b["yb"].at[low], b["home"].at[low], at_offset(0, *place(low)[1:], sign=-1))

    def ly_copy(low):
        return pair("ly", low, b["lyb"].at[low], b["lhome"].at[low], at_offset(0, *place(low)[1:], sign=-1))

    for side in range(2):
        for copy in a_copies(side, 0) + a_copies(side, 1):
            copy.wait_recv()
    for dz in BACK_ORDER:
        for half in range(2):
            for copy in b_copies(half, dz):
                copy.wait_recv()

            def step(low, carry):
                index = dz * 8 + half * 4 + low
                rows, column = part_of(0, index)
                plain = to_column(b["al_in"][1 - half, pl.ds(dz * 8 + low, 1)])
                joined = to_column(b["bl_in"][half, pl.ds(dz * 8 + low, 1)])
                out, lse = merge(
                    [
                        (rows.astype(F32), column),
                        (b["a_in"][1 - half, dz * 4 + low].astype(F32), plain),
                        (b["b_in"][half, dz * 4 + low].astype(F32), joined),
                    ]
                )
                b["h_out" if dz else "h_in"][index] = out.astype(BF)
                b["l_out" if dz else "l_in"][dz, half * 4 + low] = to_row(lse)
                return carry

            lax.fori_loop(0, 4, step, 0, unroll=4)
        if dz:
            hz_copy(dz).start()
            lz_copy(dz).start()
    for dz in range(1, 4):
        hz_copy(dz).wait_recv()
        lz_copy(dz).wait_recv()
    for low in (4, 5, 6, 7, 2, 3, 1, 0):
        target, ltarget = ("yb", "lyb") if low else ("home", "lhome")
        for branch in range(2):
            slot = jnp.clip(b["order_s"][32 + 2 * low + branch, 0], 0, 15)
            away = lax.rem(slot // 4 - z + 4, 4)
            b[target][low, branch] = b["h_in"][away * 8 + low]
            b[ltarget][low, branch] = b["l_in"][away, low]
        if low:
            hy_copy(low).start()
            ly_copy(low).start()
    for low in range(1, 8):
        hy_copy(low).wait_recv()
        ly_copy(low).wait_recv()

    for branch in range(2):
        def step(low, carry):
            dy = low // 2
            dc = low % 2
            head = lax.rem(y + dy, 4) * 2 + lax.rem(c + dc, 2)
            lse = to_column(b["lhome"][low, branch])
            out, _ = merge(
                [(b["home"][low, branch].astype(F32), lse), (b["own_o"][branch, head], b["own_l"][branch, head])]
            )
            o_ref[branch, :, pl.ds(pl.multiple_of(head * 16, 16), 16), :] = out.astype(BF).reshape(4, 16, HD)
            return carry

        lax.fori_loop(0, 8, step, 0, unroll=4)

    for dz in range(1, 4):
        for copy in (qz_copy, mz_copy, hz_copy, lz_copy):
            copy(dz).wait_send()
    for low in range(1, 8):
        for copy in (qy_copy, my_copy, hy_copy, ly_copy):
            copy(low).wait_send()
    fm_copy().wait_send()
    for side in range(2):
        xm_copy(side).wait_send()
        for copy in a_copies(side, 0) + a_copies(side, 1):
            copy.wait_send()
        for dz in range(4):
            for copy in (x_copy(dz, side), f_copy(dz, side)) + c_copies(side, dz) + b_copies(side, dz):
                copy.wait_send()


def scratch_shapes():
    dma = pltpu.SemaphoreType.DMA
    vmem = pltpu.VMEM
    shapes = {
        "q_v": vmem((2, 4, 128, HD), BF),
        "pk_v": vmem((4, 1024, HD), BF),
        "kt": vmem((4, HD, 1024), BF),
        "va": vmem((4, 1024, 2 * HD), BF),
        "sk_v": vmem((2, 512, 8, HD), BF),
        "sv_v": vmem((2, 512, 8, HD), BF),
        "nk_v": vmem((2, 4, 8, HD), BF),
        "nv_v": vmem((2, 4, 8, HD), BF),
        "wide_k": vmem((4104, HD), F32),
        "wide_v": vmem((4104, HD), F32),
        "wide_nk": vmem((40, HD), F32),
        "wide_nv": vmem((40, HD), F32),
        "own_o": vmem((2, 8, ROWS, HD), F32),
        "own_l": vmem((2, 8, ROWS, HD), F32),
        "qy": vmem((8, 2, 4, 16, HD), BF),
        "zb": vmem((4, 8, ROWS, HD), BF),
        "mb": vmem((2, 1, 128), jnp.int32),
        "my": vmem((8, 2, 1, 128), jnp.int32),
        "mz": vmem((4, 8, 1, 128), jnp.int32),
        "order_v": vmem((48, 128), jnp.int32),
        "order_s": pltpu.SMEM((48, 128), jnp.int32),
        "l_out": vmem((4, 8, 1, 128), F32),
        "l_in": vmem((4, 8, 1, 128), F32),
        "yb": vmem((8, 2, ROWS, HD), BF),
        "home": vmem((8, 2, ROWS, HD), BF),
        "lyb": vmem((8, 2, 1, 128), F32),
        "lhome": vmem((8, 2, 1, 128), F32),
        "a_out": vmem((2, 16, ROWS, HD), BF),
        "a_in": vmem((2, 16, ROWS, HD), BF),
        "c_out": vmem((2, 16, ROWS, HD), BF),
        "c_in": vmem((2, 16, ROWS, HD), BF),
        "b_out": vmem((2, 16, ROWS, HD), BF),
        "b_in": vmem((2, 16, ROWS, HD), BF),
        "h_out": vmem((SLOTS, ROWS, HD), BF),
        "h_in": vmem((SLOTS, ROWS, HD), BF),
        "local_sem": dma((8,)),
    }
    for name in ("al", "cl", "bl"):
        shapes[name + "_out"] = vmem((2, 32, 128), F32)
        shapes[name + "_in"] = vmem((2, 32, 128), F32)
    for number in range(4):
        shapes["qx%d" % number] = vmem((SLOTS, ROWS, HD), BF)
        shapes["mx%d" % number] = vmem((4, 8, 1, 128), jnp.int32)
        shapes["ot%d" % number] = vmem((2 * TILES, ROWS, HD), BF)
        shapes["lt%d" % number] = vmem((2 * TILES, ROWS, HD), F32)
    for name, count in (
        ("qz", (4,)), ("mz", (4,)), ("qy", (8,)), ("my", (8,)), ("x", (2, 4)), ("xm", (2,)), ("f", (2, 4)),
        ("fm", (1,)), ("a", (2, 2)), ("al", (2, 2)), ("c", (2, 4)), ("cl", (2, 4)), ("b", (2, 4)), ("bl", (2, 4)),
        ("hy", (8,)), ("ly", (8,)), ("hz", (4,)), ("lz", (4,)),
    ):
        shapes[name + "_send"] = dma(count)
        shapes[name + "_recv"] = dma(count)
    return shapes


NAMES = tuple(scratch_shapes())


def body(
    queries, prefix_keys, prefix_values, suffix_keys, suffix_values, new_keys, new_values, suffix_lengths, branch_prefix,
    prefix_slot,
):
    smem = pl.BlockSpec(memory_space=pltpu.SMEM)
    hbm = pl.BlockSpec(memory_space=pl.ANY)
    return pl.pallas_call(
        kernel,
        out_shape=jax.ShapeDtypeStruct(queries.shape, BF),
        in_specs=[smem] * 3 + [hbm] * 7,
        out_specs=pl.BlockSpec(memory_space=pltpu.VMEM),
        scratch_shapes=list(scratch_shapes().values()),
        compiler_params=pltpu.CompilerParams(collective_id=0, has_side_effects=True, vmem_limit_bytes=60 << 20),
        name="attend",
    )(
        branch_prefix, prefix_slot, suffix_lengths, queries, prefix_keys[:, 0], prefix_values[:, 0], suffix_keys,
        suffix_values, new_keys, new_values,
    )


def solution(mesh):
    both = P(("grp", "shard"), None, None, None)
    prefix = P("grp", "shard", None, None)
    flat = P(("grp", "shard"))
    return jax.shard_map(
        body,
        mesh=mesh,
        in_specs=(both, prefix, prefix, both, both, both, both, flat, flat, P()),
        out_specs=both,
        check_vma=False,
    )
```
